512 devices in a mesh: ctx: 64 (over y, z), tp: 8 (over x, core).
Axes of the slice: x: 4, y: 4, z: 16, core: 2. Of those that a mesh axis runs over, the one named last changes fastest.
Arguments:
- lin_query: bfloat16 [8192, 4096], P('ctx', 'tp'), may hold values from -6 to 6
- lin_key: bfloat16 [8192, 4096], P('ctx', 'tp'), may hold values from -6 to 6
- lin_value: bfloat16 [8192, 4096], P('ctx', 'tp'), may hold values from -6 to 6
- lin_cotangent: bfloat16 [8192, 4096], P('ctx', 'tp'), may hold values from -6 to 6
- soft_query: bfloat16 [8192, 4096], P('ctx', 'tp'), may hold values from -200 to 200
- soft_key: bfloat16 [8192, 1024], P('ctx', 'tp'), may hold values from -200 to 200
- soft_value: bfloat16 [8192, 1024], P('ctx', 'tp'), may hold values from -6 to 6
- doc_start: int32 [8192], P('ctx'), may hold values from 0 to 8191, as said below
Outputs:
- lin_out: bfloat16 [8192, 4096], P('ctx', 'tp')
- grad_query: bfloat16 [8192, 4096], P('ctx', 'tp')
- grad_key: bfloat16 [8192, 4096], P('ctx', 'tp')
- grad_value: bfloat16 [8192, 4096], P('ctx', 'tp')
- soft_out: bfloat16 [8192, 4096], P('ctx', 'tp')
The draws below stay inside these ranges and needn't reach their ends.
Inputs may be any that keep to these rules, and one draw needn't show every extreme that they name: doc_start[i] <= i, doc_start never falls along the sequence, doc_start[0] = 0, doc_start[i] equals i or doc_start[i - 1], and a document of one position starts at position 8191.
All inputs are finite; a program needn't handle non-finite values.
Results may differ from the reference program's by a relative error of at most 0.011.
Values may be sent and summed in bfloat16 or wider, within the bound.
No kernel may reach another device: no remote copies, remote signals or barrier semaphores. Data moves between devices by JAX's collectives and lax.ppermute only.
A program may use at most 128 MiB of HBM per device.

```python
import math
import jax
import jax.numpy as jnp
from jax import lax

HD = 128
LH = 32
SH = 32
KVH = 8
T_DEV = 128
SEQ = 8192
DOC_MEAN = 2048
N_CTX = 64


def paired_draw(key):
    query_key, key_key = jax.random.split(jax.random.fold_in(key, 17), 2)
    queries = jax.random.normal(query_key, (SEQ, SH, HD), jnp.float32)
    keys = jax.random.normal(key_key, (SEQ, KVH, HD), jnp.float32)
    return (queries.reshape(SEQ, SH * HD), keys.reshape(SEQ, KVH * HD))


def draw_soft_query(key, part):
    return paired_draw(key)[0].astype(jnp.bfloat16)


def draw_soft_key(key, part):
    return paired_draw(key)[1].astype(jnp.bfloat16)


def draw_doc_start(key, part):
    marks = jax.random.randint(jax.random.fold_in(key, 5), (SEQ,), 0, DOC_MEAN)
    positions = jnp.arange(SEQ, dtype=jnp.int32)
    quiet = (positions > SEQ // 4) & (positions < 3 * SEQ // 4 + T_DEV)
    opens = (marks == 0) & jnp.logical_not(quiet) | (positions == 0) | (positions == SEQ - 1)
    begins = jnp.where(opens, positions, 0).astype(jnp.int32)
    return lax.cummax(begins, axis=0)


def shard_levels(own_key, shape, cuts, least, largest):
    level, own = 1.0, jax.random.fold_in(own_key, 6)
    for axis_at, blocks in cuts:
        steps = jnp.exp(jax.random.uniform(jax.random.fold_in(own, axis_at), (blocks,), jnp.float32, least / len(cuts), largest / len(cuts)))
        level = level * jnp.repeat(steps, shape[axis_at] // blocks).reshape([-1 if axis == axis_at else 1 for axis in range(len(shape))])
    return level


def normal_values(stream_key, extent, width, limit, shards=(), held_as=jnp.bfloat16):
    values = width * jax.random.normal(stream_key, extent, jnp.float32)
    if shards:
        values = values * shard_levels(stream_key, extent, shards, -0.22, 0.18)
    return jnp.clip(values, -limit, limit).astype(held_as)


def setup_inputs(seed: int = 0) -> dict:
    arg_keys = jax.random.split(jax.random.key(seed), 9)
    lin_query = normal_values(arg_keys[0], (SEQ, LH * HD), 1.0, 6.0, ((0, 64), (1, 8)))
    lin_key = normal_values(arg_keys[1], (SEQ, LH * HD), 1.0, 6.0, ((0, 64), (1, 8)))
    lin_value = normal_values(arg_keys[2], (SEQ, LH * HD), 1.0, 6.0, ((0, 64), (1, 8)))
    lin_cotangent = normal_values(arg_keys[3], (SEQ, LH * HD), 1.0, 6.0, ((0, 64), (1, 8)))
    soft_query = draw_soft_query(jax.random.fold_in(arg_keys[8], 71), 0)
    soft_key = draw_soft_key(jax.random.fold_in(arg_keys[8], 71), 0)
    soft_value = normal_values(arg_keys[6], (SEQ, KVH * HD), 1.0, 6.0, ((0, 64), (1, 8)))
    doc_start = draw_doc_start(jax.random.fold_in(arg_keys[8], 71), 0)
    return {"lin_query": lin_query, "lin_key": lin_key, "lin_value": lin_value, "lin_cotangent": lin_cotangent, "soft_query": soft_query, "soft_key": soft_key, "soft_value": soft_value, "doc_start": doc_start}


epsilon = 1e-06
highest = lax.Precision.HIGHEST
floor_score = -1e+30

def rounded(value):
    return lax.optimization_barrier(value.astype(jnp.bfloat16)).astype(jnp.float32)

def causal_scores(left, right, lower):
    raw = jnp.einsum('thd,shd->hts', left, right, precision=highest)
    return rounded(jnp.where(lower[None], raw, 0.0))

def outer_sum(left, right):
    return jnp.einsum('thd,the->hde', left, right, precision=highest)

def lightning(lin_query, lin_key, lin_value, lin_cotangent):
    shape = (N_CTX, T_DEV, LH, HD)
    queries = lin_query.astype(jnp.float32).reshape(shape)
    keys = lin_key.astype(jnp.float32).reshape(shape)
    values = lin_value.astype(jnp.float32).reshape(shape)
    lower = jnp.tril(jnp.ones((T_DEV, T_DEV), dtype=bool))
    zero_state = jnp.zeros((LH, HD, HD), jnp.float32)

    def forward(state, item):
        query_block, key_block, value_block = item
        weights = causal_scores(query_block, key_block, lower)
        mixed = jnp.einsum('hts,shd->thd', weights, value_block, precision=highest)
        mixed = mixed + jnp.einsum('thd,hde->the', query_block, state, precision=highest)
        return (state + outer_sum(key_block, value_block), mixed)
    unused, mixed = lax.scan(forward, zero_state, (queries, keys, values))
    mixed = mixed.reshape(SEQ, LH * HD)
    scale = lax.rsqrt(lax.optimization_barrier(jnp.mean(mixed * mixed, axis=1)) + epsilon)
    normed = mixed * scale[:, None]
    lin_out = normed.astype(jnp.bfloat16)
    grad = lin_cotangent.astype(jnp.float32)
    inner = lax.optimization_barrier(jnp.mean(grad * normed, axis=1))
    grad_mix = rounded(scale[:, None] * (grad - normed * inner[:, None])).reshape(shape)

    def query_pass(state, item):
        key_block, value_block, grad_block = item
        grad_scores = causal_scores(grad_block, value_block, lower)
        grad_q = jnp.einsum('hts,shd->thd', grad_scores, key_block, precision=highest)
        grad_q = grad_q + jnp.einsum('the,hde->thd', grad_block, state, precision=highest)
        return (state + outer_sum(key_block, value_block), grad_q)
    unused, grad_q = lax.scan(query_pass, zero_state, (keys, values, grad_mix))

    def key_pass(state, item):
        query_block, key_block, value_block, grad_block = item
        weights = causal_scores(query_block, key_block, lower)
        grad_scores = causal_scores(grad_block, value_block, lower)
        grad_k = jnp.einsum('hts,thd->shd', grad_scores, query_block, precision=highest)
        grad_k = grad_k + jnp.einsum('she,hde->shd', value_block, state, precision=highest)
        grad_v = jnp.einsum('hts,thd->shd', weights, grad_block, precision=highest)
        grad_v = grad_v + jnp.einsum('shd,hde->she', key_block, state, precision=highest)
        return (state + outer_sum(query_block, grad_block), (grad_k, grad_v))
    unused, (grad_k, grad_v) = lax.scan(key_pass, zero_state, (queries, keys, values, grad_mix), reverse=True)
    grad_query = grad_q.reshape(SEQ, LH * HD).astype(jnp.bfloat16)
    grad_key = grad_k.reshape(SEQ, LH * HD).astype(jnp.bfloat16)
    grad_value = grad_v.reshape(SEQ, LH * HD).astype(jnp.bfloat16)
    return (lin_out, grad_query, grad_key, grad_value)

def softmax_layer(soft_query, soft_key, soft_value, doc_start):
    group = SH // KVH
    scale = 1.0 / math.sqrt(HD)
    queries = soft_query.astype(jnp.float32).reshape(N_CTX, T_DEV, KVH, group, HD)
    starts = doc_start.reshape(N_CTX, T_DEV)
    keys = soft_key.astype(jnp.float32).reshape(SEQ, KVH, HD)
    values = soft_value.astype(jnp.float32).reshape(SEQ, KVH, HD)
    key_pos = jnp.arange(SEQ, dtype=jnp.int32)
    blocks = jnp.arange(N_CTX, dtype=jnp.int32)

    def one_block(item):
        query_block, start_block, index = item
        query_pos = index * T_DEV + jnp.arange(T_DEV, dtype=jnp.int32)
        allowed = (key_pos[None, :] <= query_pos[:, None]) & (key_pos[None, :] >= start_block[:, None])
        scores = jnp.einsum('tkgd,nkd->kgtn', query_block, keys, precision=highest) * scale
        scores = jnp.where(allowed, scores, floor_score)
        top = lax.optimization_barrier(jnp.max(scores, axis=-1))
        weights = jnp.where(allowed, jnp.exp(scores - top[..., None]), 0.0)
        total = lax.optimization_barrier(jnp.sum(weights, axis=-1))
        mixed = jnp.einsum('kgtn,nkd->kgtd', rounded(weights), values, precision=highest)
        out = mixed / total[..., None]
        return jnp.transpose(out, (2, 0, 1, 3)).reshape(T_DEV, SH * HD).astype(jnp.bfloat16)
    result = lax.map(one_block, (queries, starts, blocks))
    return result.reshape(SEQ, SH * HD)

def reference(lin_query, lin_key, lin_value, lin_cotangent, soft_query, soft_key, soft_value, doc_start):
    lin_out, grad_query, grad_key, grad_value = lightning(lin_query, lin_key, lin_value, lin_cotangent)
    soft_out = softmax_layer(soft_query, soft_key, soft_value, doc_start)
    return (lin_out, grad_query, grad_key, grad_value, soft_out)
```

```python
import functools
import math

import jax
import jax.numpy as jnp
from jax import lax
from jax.experimental import pallas as pl
from jax.experimental.pallas import tpu as pltpu
from jax.sharding import PartitionSpec as P

HD = 128
LH = 32
SH = 32
KVH = 8
T = 128
HERE = 4
TP = 8
NY = 4
NZ = 16
PIECE = HERE * HD // NZ
CHUNK = 4

epsilon = 1e-06
floor_score = -1e30
bf16 = jnp.bfloat16
f32 = jnp.float32

z_groups = [[y * NZ + z for z in range(NZ)] for y in range(NY)]


def y_shift(step):
    return [(i, i + NZ * step) for i in range(NY * NZ) if 0 <= i + NZ * step < NY * NZ]


def dot(a, b, contract_a, contract_b):
    return lax.dot_general(
        a, b, (((contract_a,), (contract_b,)), ((), ())), preferred_element_type=f32
    )


def call(kernel, outs, *args, flops=1e8, name=None, vmem=48 * 2**20, scratch=(), smem=()):
    size = sum(a.size * a.dtype.itemsize for a in args)
    size += sum(math.prod(s) * jnp.dtype(d).itemsize for s, d in outs)
    specs = [
        pl.BlockSpec(memory_space=pltpu.SMEM if i in smem else pltpu.VMEM)
        for i in range(len(args))
    ]
    out = pl.pallas_call(
        kernel,
        out_shape=[jax.ShapeDtypeStruct(s, d) for s, d in outs],
        in_specs=specs,
        out_specs=[pl.BlockSpec(memory_space=pltpu.VMEM) for _ in outs],
        scratch_shapes=list(scratch),
        compiler_params=pltpu.CompilerParams(vmem_limit_bytes=vmem),
        cost_estimate=pl.CostEstimate(flops=int(flops), bytes_accessed=size, transcendentals=0),
        name=name,
    )(*args)
    return out


def head(ref, h):
    return ref[:, h * HD : (h + 1) * HD]


def state_of(ref, h):
    per = HD // PIECE
    return ref[h * per : (h + 1) * per].reshape(HD, HD)


def put_state(ref, h, value):
    per = HD // PIECE
    ref[h * per : (h + 1) * per] = value.astype(bf16).reshape(per, PIECE, HD)


def lower_triangle():
    rows = lax.broadcasted_iota(jnp.int32, (T, T), 0)
    cols = lax.broadcasted_iota(jnp.int32, (T, T), 1)
    return cols <= rows


def own_kernel(k, v, sk, sv, own, kv):
    kv[0] = sk[...]
    kv[1] = sv[...]
    for h in range(HERE):
        put_state(own, h, dot(head(k, h), head(v, h), 0, 0))


def local_kernel(q, k, v, weights, local):
    lower = lower_triangle()
    for h in range(HERE):
        w = jnp.where(lower, dot(head(q, h), head(k, h), 1, 1), 0.0).astype(bf16)
        weights[h] = w
        local[:, h * HD : (h + 1) * HD] = dot(w, head(v, h), 1, 0)


def total_kernel(r, tot):
    acc = r[0].astype(f32)
    for i in range(1, NZ):
        acc = acc + r[i].astype(f32)
    tot[...] = acc.astype(bf16)


def carry_kernel(reverse, r, a, b, c, out):
    acc = a[...].astype(f32) + b[...].astype(f32) + c[...].astype(f32)
    for i in reversed(range(NZ)) if reverse else range(NZ):
        out[i] = acc.astype(bf16)
        acc = acc + r[i].astype(f32)


def mix_kernel(q, g, local, s, mix, sums):
    squares = jnp.zeros((T, HD), f32)
    inner = jnp.zeros((T, HD), f32)
    for h in range(HERE):
        m = head(local, h) + dot(head(q, h), state_of(s, h), 1, 0)
        mix[:, h * HD : (h + 1) * HD] = m
        squares = squares + m * m
        inner = inner + m * head(g, h).astype(f32)
    lane = lax.broadcasted_iota(jnp.int32, (T, HD), 1)
    both = jnp.where(
        lane == 0,
        jnp.sum(squares, axis=1, keepdims=True),
        jnp.where(lane == 1, jnp.sum(inner, axis=1, keepdims=True), 0.0),
    )
    rows = jnp.transpose(both)[0:8]
    for i in range(TP):
        sums[i] = rows


def norm_kernel(q, g, mix, sums, lin_out, grad_mix, own):
    rows = sums[0]
    for i in range(1, TP):
        rows = rows + sums[i]
    cols = jnp.transpose(jnp.concatenate([rows, jnp.zeros((T - 8, HD), f32)], axis=0))
    scale = lax.rsqrt(cols[:, 0:1] / (LH * HD) + epsilon)
    c = scale * cols[:, 1:2] / (LH * HD)
    for h in range(HERE):
        normed = head(mix, h) * scale
        lin_out[:, h * HD : (h + 1) * HD] = normed.astype(bf16)
        gm = (scale * (head(g, h).astype(f32) - normed * c)).astype(bf16)
        grad_mix[:, h * HD : (h + 1) * HD] = gm
        put_state(own, h, dot(head(q, h), gm, 0, 0))


def inside_kernel(q, k, v, gm, weights, s, grad_q, part_k, part_v):
    lower = lower_triangle()
    for h in range(HERE):
        at = slice(h * HD, (h + 1) * HD)
        gs = jnp.where(lower, dot(head(gm, h), head(v, h), 1, 1), 0.0).astype(bf16)
        gq = dot(gs, head(k, h), 1, 0) + dot(head(gm, h), state_of(s, h), 1, 1)
        grad_q[:, at] = gq.astype(bf16)
        part_k[:, at] = dot(gs, head(q, h), 0, 0)
        part_v[:, at] = dot(weights[h], head(gm, h), 0, 0)


def final_kernel(k, v, part_k, part_v, a, grad_k, grad_v):
    for h in range(HERE):
        at = slice(h * HD, (h + 1) * HD)
        later = state_of(a, h)
        grad_k[:, at] = (head(part_k, h) + dot(head(v, h), later, 1, 1)).astype(bf16)
        grad_v[:, at] = (head(part_v, h) + dot(head(k, h), later, 1, 0)).astype(bf16)


def soft_kernel(q, kv, doc_row, doc, out, qs, top, total, acc):
    me = lax.axis_index("ctx")
    my_y = me // NZ
    keys = CHUNK * T
    width = HERE * T
    factor = math.log2(math.e) / math.sqrt(HD)
    for h in range(HERE):
        qs[h * T : (h + 1) * T] = head(q, h)
    top[...] = jnp.full((1, width), floor_score, f32)
    total[...] = jnp.zeros((1, width), f32)
    acc[...] = jnp.zeros((HD, width), f32)
    first_chunk = doc[0] // keys
    my_chunk = me // CHUNK
    last_start = doc[T - 1]

    def visit(chunk, masked):
        block = chunk * CHUNK
        slot = my_y - block // NZ
        z0 = lax.rem(block, NZ)
        k = kv[pl.ds(z0, CHUNK), slot, 0].reshape(keys, HD)
        v = kv[pl.ds(z0, CHUNK), slot, 1].reshape(keys, HD)
        scores = dot(k, qs[...], 1, 1)
        if masked:
            key_pos = chunk * keys + lax.broadcasted_iota(jnp.int32, (keys, width), 0)
            query_pos = me * T + lax.rem(
                lax.broadcasted_iota(jnp.int32, (1, width), 1), jnp.int32(T)
            )
            starts = jnp.concatenate([doc_row[...]] * HERE, axis=1)
            allowed = (key_pos <= query_pos) & (key_pos >= starts)
            scores = jnp.where(allowed, scores, 2 * floor_score)
        old_top = top[...]
        new_top = jnp.maximum(old_top, jnp.max(scores, axis=0, keepdims=True))
        probs = jnp.exp2((scores - new_top) * factor)
        shrink = jnp.exp2((old_top - new_top) * factor)
        top[...] = new_top
        total[...] = shrink * total[...] + jnp.sum(probs, axis=0, keepdims=True)
        acc[...] = shrink * acc[...] + dot(v, probs.astype(bf16), 0, 0)

    def step(chunk, carry):
        clear = (chunk < my_chunk) & (chunk * keys >= last_start)

        @pl.when(clear)
        def _():
            visit(chunk, False)

        @pl.when(jnp.logical_not(clear))
        def _():
            visit(chunk, True)

        return carry

    lax.fori_loop(first_chunk, my_chunk + 1, step, 0)
    result = acc[...] / total[...]
    for h in range(HERE):
        out[:, h * HD : (h + 1) * HD] = jnp.transpose(result[:, h * T : (h + 1) * T]).astype(bf16)


def carried_in(own, reverse):
    pieces = (NZ, PIECE, HD)
    tag = "later" if reverse else "earlier"
    swap = functools.partial(
        lax.all_to_all,
        axis_name="ctx",
        split_axis=0,
        concat_axis=0,
        tiled=True,
        axis_index_groups=z_groups,
    )
    got = swap(own)
    (line,) = call(total_kernel, [((PIECE, HD), bf16)], got, flops=1e5, name=tag + "_total")
    sign = -1 if reverse else 1
    rows = [lax.ppermute(line, "ctx", y_shift(sign * s)) for s in (1, 2, 3)]
    (carried,) = call(
        functools.partial(carry_kernel, reverse),
        [(pieces, bf16)],
        got,
        *rows,
        flops=1e5,
        name=tag + "_carry",
    )
    return swap(carried)


def on_device(
    lin_query, lin_key, lin_value, lin_cotangent, soft_query, soft_key, soft_value, doc_start
):
    q, k, v, g = lin_query, lin_key, lin_value, lin_cotangent
    wide = (T, HERE * HD)
    states = (NZ, PIECE, HD)
    squares = (HERE, T, T)
    own, kv = call(
        own_kernel,
        [(states, bf16), ((2, T, HD), bf16)],
        k,
        v,
        soft_key,
        soft_value,
        name="own_state",
    )
    slots = [kv] + [lax.ppermute(kv, "ctx", y_shift(s)) for s in (1, 2, 3)]
    all_kv = lax.all_gather(jnp.stack(slots), "ctx", axis_index_groups=z_groups)
    weights, local = call(
        local_kernel, [(squares, bf16), (wide, f32)], q, k, v, name="local"
    )
    earlier = carried_in(own, False)
    mix, sums = call(
        mix_kernel, [(wide, f32), ((TP, 8, HD), f32)], q, g, local, earlier, name="mix"
    )
    sums = lax.all_to_all(sums, "tp", 0, 0, tiled=True)
    lin_out, gm, own_adjoint = call(
        norm_kernel,
        [(wide, bf16), (wide, bf16), (states, bf16)],
        q,
        g,
        mix,
        sums,
        name="norm",
    )
    later = carried_in(own_adjoint, True)
    grad_query, part_k, part_v = call(
        inside_kernel,
        [(wide, bf16), (wide, f32), (wide, f32)],
        q,
        k,
        v,
        gm,
        weights,
        earlier,
        name="inside",
    )
    grad_key, grad_value = call(
        final_kernel, [(wide, bf16), (wide, bf16)], k, v, part_k, part_v, later, name="final"
    )
    (soft_out,) = call(
        soft_kernel,
        [(wide, bf16)],
        soft_query,
        all_kv,
        doc_start.reshape(1, T),
        doc_start,
        smem=(3,),
        flops=1e9,
        scratch=[
            pltpu.VMEM((HERE * T, HD), bf16),
            pltpu.VMEM((1, HERE * T), f32),
            pltpu.VMEM((1, HERE * T), f32),
            pltpu.VMEM((HD, HERE * T), f32),
        ],
        name="soft",
    )
    return (lin_out, grad_query, grad_key, grad_value, soft_out)


def solution(mesh):
    wide = P("ctx", "tp")
    return jax.shard_map(
        on_device,
        mesh=mesh,
        in_specs=(wide,) * 7 + (P("ctx"),),
        out_specs=(wide,) * 5,
        check_vma=False,
    )
```

```python
import functools
import math

import jax
import jax.numpy as jnp
from jax import lax
from jax.experimental import pallas as pl
from jax.experimental.pallas import tpu as pltpu
from jax.sharding import PartitionSpec as P

HD = 128
LH = 32
SH = 32
KVH = 8
T = 128
HERE = 4
TP = 8
NY = 4
NZ = 16
PIECE = HERE * HD // NZ
CHUNK = 4

BIG = 60 * 2**20
COST = dict(own=1e8, local=1e8, total=1e10, carry=1e10, mix=1.6e10, norm=1.6e10, inside=1e8, final=1e8, soft=1e8)

epsilon = 1e-06
floor_score = -1e30
bf16 = jnp.bfloat16
f32 = jnp.float32

z_groups = [[y * NZ + z for z in range(NZ)] for y in range(NY)]


def y_shift(step):
    return [(i, i + NZ * step) for i in range(NY * NZ) if 0 <= i + NZ * step < NY * NZ]


def dot(a, b, contract_a, contract_b):
    return lax.dot_general(
        a, b, (((contract_a,), (contract_b,)), ((), ())), preferred_element_type=f32
    )


def call(kernel, outs, *args, flops=1e8, name=None, vmem=16 * 2**20, scratch=(), smem=(), far=(), far_out=()):
    size = sum(a.size * a.dtype.itemsize for a in args)
    size += sum(math.prod(s) * jnp.dtype(d).itemsize for s, d in outs)
    specs = [
        pl.BlockSpec(memory_space=pltpu.SMEM if i in smem else pltpu.HBM if i in far else pltpu.VMEM)
        for i in range(len(args))
    ]
    out = pl.pallas_call(
        kernel,
        out_shape=[jax.ShapeDtypeStruct(s, d) for s, d in outs],
        in_specs=specs,
        out_specs=[
            pl.BlockSpec(memory_space=pltpu.HBM if i in far_out else pltpu.VMEM)
            for i in range(len(outs))
        ],
        scratch_shapes=list(scratch),
        compiler_params=pltpu.CompilerParams(vmem_limit_bytes=vmem),
        cost_estimate=pl.CostEstimate(flops=int(flops), bytes_accessed=size, transcendentals=0),
        name=name,
    )(*args)
    return out


def head(ref, h):
    return ref[:, h * HD : (h + 1) * HD]


def state_of(ref, h):
    per = HD // PIECE
    return ref[h * per : (h + 1) * per].reshape(HD, HD)


def put_state(ref, h, value):
    per = HD // PIECE
    ref[h * per : (h + 1) * per] = value.astype(bf16).reshape(per, PIECE, HD)


def lower_triangle():
    rows = lax.broadcasted_iota(jnp.int32, (T, T), 0)
    cols = lax.broadcasted_iota(jnp.int32, (T, T), 1)
    return cols <= rows


def own_kernel(k_far, v_far, sk_far, sv_far, own, kv, k, v, sem):
    moves = [(k_far, k), (v_far, v), (sk_far, kv.at[0]), (sv_far, kv.at[1])]
    copies = [pltpu.make_async_copy(a, b, sem.at[i]) for i, (a, b) in enumerate(moves)]
    for copy in copies:
        copy.start()
    copies[0].wait()
    copies[1].wait()
    for h in range(HERE):
        put_state(own, h, dot(head(k, h), head(v, h), 0, 0))
    copies[2].wait()
    copies[3].wait()


def local_kernel(q_far, g_far, k, v, weights, local, q, g, sem):
    moves = [(q_far, q), (g_far, g)]
    copies = [pltpu.make_async_copy(a, b, sem.at[i]) for i, (a, b) in enumerate(moves)]
    for copy in copies:
        copy.start()
    for copy in copies:
        copy.wait()
    lower = lower_triangle()
    for h in range(HERE):
        w = jnp.where(lower, dot(head(q, h), head(k, h), 1, 1), 0.0).astype(bf16)
        weights[h] = w
        local[:, h * HD : (h + 1) * HD] = dot(w, head(v, h), 1, 0)


def total_kernel(r, tot):
    acc = r[0].astype(f32)
    for i in range(1, NZ):
        acc = acc + r[i].astype(f32)
    tot[...] = acc.astype(bf16)


def carry_kernel(reverse, r, a, b, c, out):
    acc = a[...].astype(f32) + b[...].astype(f32) + c[...].astype(f32)
    for i in reversed(range(NZ)) if reverse else range(NZ):
        out[i] = acc.astype(bf16)
        acc = acc + r[i].astype(f32)


def mix_kernel(q, g, local, s, mix, sums):
    squares = jnp.zeros((T, HD), f32)
    inner = jnp.zeros((T, HD), f32)
    for h in range(HERE):
        m = head(local, h) + dot(head(q, h), state_of(s, h), 1, 0)
        mix[:, h * HD : (h + 1) * HD] = m
        squares = squares + m * m
        inner = inner + m * head(g, h).astype(f32)
    lane = lax.broadcasted_iota(jnp.int32, (T, HD), 1)
    both = jnp.where(
        lane == 0,
        jnp.sum(squares, axis=1, keepdims=True),
        jnp.where(lane == 1, jnp.sum(inner, axis=1, keepdims=True), 0.0),
    )
    rows = jnp.transpose(both)[0:8]
    for i in range(TP):
        sums[i] = rows


def norm_kernel(q, g, mix, sums, lin_out, grad_mix, own):
    rows = sums[0]
    for i in range(1, TP):
        rows = rows + sums[i]
    cols = jnp.transpose(jnp.concatenate([rows, jnp.zeros((T - 8, HD), f32)], axis=0))
    scale = lax.rsqrt(cols[:, 0:1] / (LH * HD) + epsilon)
    c = scale * cols[:, 1:2] / (LH * HD)
    for h in range(HERE):
        normed = head(mix, h) * scale
        lin_out[:, h * HD : (h + 1) * HD] = normed.astype(bf16)
        gm = (scale * (head(g, h).astype(f32) - normed * c)).astype(bf16)
        grad_mix[:, h * HD : (h + 1) * HD] = gm
        put_state(own, h, dot(head(q, h), gm, 0, 0))


def inside_kernel(q, k, v, gm, weights, s, grad_q, part_k, part_v):
    lower = lower_triangle()
    for h in range(HERE):
        at = slice(h * HD, (h + 1) * HD)
        gs = jnp.where(lower, dot(head(gm, h), head(v, h), 1, 1), 0.0).astype(bf16)
        gq = dot(gs, head(k, h), 1, 0) + dot(head(gm, h), state_of(s, h), 1, 1)
        grad_q[:, at] = gq.astype(bf16)
        part_k[:, at] = dot(gs, head(q, h), 0, 0)
        part_v[:, at] = dot(weights[h], head(gm, h), 0, 0)


def final_kernel(k, v, part_k, part_v, a, after, grad_k, grad_v):
    del after
    for h in range(HERE):
        at = slice(h * HD, (h + 1) * HD)
        later = state_of(a, h)
        grad_k[:, at] = (head(part_k, h) + dot(head(v, h), later, 1, 1)).astype(bf16)
        grad_v[:, at] = (head(part_v, h) + dot(head(k, h), later, 1, 0)).astype(bf16)


def soft_kernel(q_far, kv_far, doc_row, doc, out, ended, q, kv, qs, top, total, acc, sem, kv_sem):
    me = lax.axis_index("ctx")
    my_y = me // NZ
    keys = CHUNK * T
    width = HERE * T
    factor = math.log2(math.e) / math.sqrt(HD)
    first_chunk = doc[0] // keys
    my_chunk = me // CHUNK
    last_start = doc[T - 1]

    def fetch(chunk):
        block = chunk * CHUNK
        source = kv_far.at[pl.ds(lax.rem(block, NZ), CHUNK), my_y - block // NZ]
        return pltpu.make_async_copy(source, kv.at[chunk], kv_sem.at[chunk])

    q_copy = pltpu.make_async_copy(q_far, q, sem)
    q_copy.start()

    def ask(chunk, carry):
        fetch(chunk).start()
        return carry

    lax.fori_loop(first_chunk, my_chunk + 1, ask, 0)
    q_copy.wait()
    for h in range(HERE):
        qs[h * T : (h + 1) * T] = head(q, h)
    top[...] = jnp.full((1, width), floor_score, f32)
    total[...] = jnp.zeros((1, width), f32)
    acc[...] = jnp.zeros((HD, width), f32)

    def visit(chunk, masked):
        k = kv[chunk, :, 0].reshape(keys, HD)
        v = kv[chunk, :, 1].reshape(keys, HD)
        scores = dot(k, qs[...], 1, 1)
        if masked:
            key_pos = chunk * keys + lax.broadcasted_iota(jnp.int32, (keys, width), 0)
            query_pos = me * T + lax.rem(
                lax.broadcasted_iota(jnp.int32, (1, width), 1), jnp.int32(T)
            )
            starts = jnp.concatenate([doc_row[...]] * HERE, axis=1)
            allowed = (key_pos <= query_pos) & (key_pos >= starts)
            scores = jnp.where(allowed, scores, 2 * floor_score)
        old_top = top[...]
        new_top = jnp.maximum(old_top, jnp.max(scores, axis=0, keepdims=True))
        probs = jnp.exp2((scores - new_top) * factor)
        shrink = jnp.exp2((old_top - new_top) * factor)
        top[...] = new_top
        total[...] = shrink * total[...] + jnp.sum(probs, axis=0, keepdims=True)
        acc[...] = shrink * acc[...] + dot(v, probs.astype(bf16), 0, 0)

    def step(chunk, carry):
        fetch(chunk).wait()
        clear = (chunk < my_chunk) & (chunk * keys >= last_start)

        @pl.when(clear)
        def _():
            visit(chunk, False)

        @pl.when(jnp.logical_not(clear))
        def _():
            visit(chunk, True)

        return carry

    lax.fori_loop(first_chunk, my_chunk + 1, step, 0)
    ended[...] = jnp.zeros((8, HD), f32)
    result = acc[...] / total[...]
    for h in range(HERE):
        out[:, h * HD : (h + 1) * HD] = jnp.transpose(result[:, h * T : (h + 1) * T]).astype(bf16)


def swap(pieces):
    return lax.all_to_all(pieces, "ctx", 0, 0, tiled=True, axis_index_groups=z_groups)


def carried_in(own, reverse):
    tag = "later" if reverse else "earlier"
    got = swap(own)
    (line,) = call(total_kernel, [((PIECE, HD), bf16)], got, flops=COST["total"], name=tag + "_total")
    sign = -1 if reverse else 1
    rows = [lax.ppermute(line, "ctx", y_shift(sign * s)) for s in (1, 2, 3)]
    (carried,) = call(
        functools.partial(carry_kernel, reverse),
        [((NZ, PIECE, HD), bf16)],
        got,
        *rows,
        flops=COST["carry"],
        name=tag + "_carry",
    )
    return swap(carried)


def on_device(
    lin_query, lin_key, lin_value, lin_cotangent, soft_query, soft_key, soft_value, doc_start
):
    wide = (T, HERE * HD)
    states = (NZ, PIECE, HD)
    squares = (HERE, T, T)
    dma = pltpu.SemaphoreType.DMA
    own, kv, k, v = call(
        own_kernel,
        [(states, bf16), ((2, T, HD), bf16), (wide, bf16), (wide, bf16)],
        lin_key,
        lin_value,
        soft_key,
        soft_value,
        far=(0, 1, 2, 3),
        flops=COST["own"],
        vmem=BIG,
        scratch=[dma((4,))],
        name="own_state",
    )
    slots = [kv] + [lax.ppermute(kv, "ctx", y_shift(s)) for s in (1, 2, 3)]
    all_kv = lax.all_gather(jnp.stack(slots), "ctx", axis_index_groups=z_groups)
    weights, local, q, g = call(
        local_kernel,
        [(squares, bf16), (wide, f32), (wide, bf16), (wide, bf16)],
        lin_query,
        lin_cotangent,
        k,
        v,
        far=(0, 1),
        scratch=[dma((2,))],
        flops=COST["local"], name="local",
    )
    earlier = carried_in(own, False)
    mix, sums = call(
        mix_kernel, [(wide, f32), ((TP, 8, HD), f32)], q, g, local, earlier, flops=COST["mix"], name="mix"
    )
    sums = lax.all_to_all(sums, "tp", 0, 0, tiled=True)
    lin_out, gm, own_adjoint = call(
        norm_kernel,
        [(wide, bf16), (wide, bf16), (states, bf16)],
        q,
        g,
        mix,
        sums,
        flops=COST["norm"], name="norm",
    )
    later = carried_in(own_adjoint, True)
    grad_query, part_k, part_v = call(
        inside_kernel,
        [(wide, bf16), (wide, f32), (wide, f32)],
        q,
        k,
        v,
        gm,
        weights,
        earlier,
        flops=COST["inside"], name="inside",
    )
    soft_out, ended = call(
        soft_kernel,
        [(wide, bf16), ((8, HD), f32)],
        soft_query,
        all_kv,
        doc_start.reshape(1, T),
        doc_start,
        smem=(3,),
        far=(0, 1),
        flops=COST["soft"],
        vmem=BIG,
        scratch=[
            pltpu.VMEM(wide, bf16),
            pltpu.VMEM((NY * NZ // CHUNK, CHUNK, 2, T, HD), bf16),
            pltpu.VMEM((HERE * T, HD), bf16),
            pltpu.VMEM((1, HERE * T), f32),
            pltpu.VMEM((1, HERE * T), f32),
            pltpu.VMEM((HD, HERE * T), f32),
            dma,
            dma((NY * NZ // CHUNK,)),
        ],
        name="soft",
    )
    grad_key, grad_value = call(
        final_kernel, [(wide, bf16), (wide, bf16)], k, v, part_k, part_v, later, ended, far=(5,), flops=COST["final"], name="final"
    )
    return (lin_out, grad_query, grad_key, grad_value, soft_out)


def solution(mesh):
    wide = P("ctx", "tp")
    return jax.shard_map(
        on_device,
        mesh=mesh,
        in_specs=(wide,) * 7 + (P("ctx"),),
        out_specs=(wide,) * 5,
        check_vma=False,
    )
```

```python
import functools
import math

import jax
import jax.numpy as jnp
from jax import lax
from jax.experimental import pallas as pl
from jax.experimental.pallas import tpu as pltpu
from jax.sharding import PartitionSpec as P

HD = 128
LH = 32
SH = 32
KVH = 8
T = 128
HERE = 4
TP = 8
NY = 4
NZ = 16
PIECE = HERE * HD // NZ
CHUNK = 4

BIG = 60 * 2**20
COST = dict(own=1e8, local=1e8, total=1e5, carry=1e5, mix=1e8, norm=1e8, inside=1e8, final=1e8, soft=1e8)

epsilon = 1e-06
floor_score = -1e30
bf16 = jnp.bfloat16
f32 = jnp.float32

y_groups = [[y * NZ + z for y in range(NY)] for z in range(NZ)]
z_groups = [[y * NZ + z for z in range(NZ)] for y in range(NY)]


def y_shift(step):
    return [(i, i + NZ * step) for i in range(NY * NZ) if 0 <= i + NZ * step < NY * NZ]


def dot(a, b, contract_a, contract_b):
    return lax.dot_general(
        a, b, (((contract_a,), (contract_b,)), ((), ())), preferred_element_type=f32
    )


def call(kernel, outs, *args, flops=1e8, name=None, vmem=16 * 2**20, scratch=(), smem=(), far=(), far_out=()):
    size = sum(a.size * a.dtype.itemsize for a in args)
    size += sum(math.prod(s) * jnp.dtype(d).itemsize for s, d in outs)
    specs = [
        pl.BlockSpec(memory_space=pltpu.SMEM if i in smem else pltpu.HBM if i in far else pltpu.VMEM)
        for i in range(len(args))
    ]
    out = pl.pallas_call(
        kernel,
        out_shape=[jax.ShapeDtypeStruct(s, d) for s, d in outs],
        in_specs=specs,
        out_specs=[
            pl.BlockSpec(memory_space=pltpu.HBM if i in far_out else pltpu.VMEM)
            for i in range(len(outs))
        ],
        scratch_shapes=list(scratch),
        compiler_params=pltpu.CompilerParams(vmem_limit_bytes=vmem),
        cost_estimate=pl.CostEstimate(flops=int(flops), bytes_accessed=size, transcendentals=0),
        name=name,
    )(*args)
    return out


def head(ref, h):
    return ref[:, h * HD : (h + 1) * HD]


def state_of(ref, h):
    per = HD // PIECE
    return ref[h * per : (h + 1) * per].reshape(HD, HD)


def put_state(ref, h, value):
    per = HD // PIECE
    ref[h * per : (h + 1) * per] = value.astype(bf16).reshape(per, PIECE, HD)


def lower_triangle():
    rows = lax.broadcasted_iota(jnp.int32, (T, T), 0)
    cols = lax.broadcasted_iota(jnp.int32, (T, T), 1)
    return cols <= rows


def own_kernel(k_far, v_far, sk_far, sv_far, own, kv, k, v, sem):
    moves = [(k_far, k), (v_far, v), (sk_far, kv.at[0, 0]), (sv_far, kv.at[0, 1])]
    copies = [pltpu.make_async_copy(a, b, sem.at[i]) for i, (a, b) in enumerate(moves)]
    for copy in copies:
        copy.start()
    copies[0].wait()
    copies[1].wait()
    for h in range(HERE):
        put_state(own, h, dot(head(k, h), head(v, h), 0, 0))
    copies[2].wait()
    copies[3].wait()
    for y in range(1, NY):
        kv[y] = kv[0]


def local_kernel(q_far, g_far, k, v, weights, local, q, g, sem):
    moves = [(q_far, q), (g_far, g)]
    copies = [pltpu.make_async_copy(a, b, sem.at[i]) for i, (a, b) in enumerate(moves)]
    for copy in copies:
        copy.start()
    for copy in copies:
        copy.wait()
    lower = lower_triangle()
    for h in range(HERE):
        w = jnp.where(lower, dot(head(q, h), head(k, h), 1, 1), 0.0).astype(bf16)
        weights[h] = w
        local[:, h * HD : (h + 1) * HD] = dot(w, head(v, h), 1, 0)


def total_kernel(r, tot):
    acc = r[0].astype(f32)
    for i in range(1, NZ):
        acc = acc + r[i].astype(f32)
    tot[...] = acc.astype(bf16)


def carry_kernel(reverse, r, a, b, c, out):
    acc = a[...].astype(f32) + b[...].astype(f32) + c[...].astype(f32)
    for i in reversed(range(NZ)) if reverse else range(NZ):
        out[i] = acc.astype(bf16)
        acc = acc + r[i].astype(f32)


def mix_kernel(q, g, local, s, mix, sums):
    squares = jnp.zeros((T, HD), f32)
    inner = jnp.zeros((T, HD), f32)
    for h in range(HERE):
        m = head(local, h) + dot(head(q, h), state_of(s, h), 1, 0)
        mix[:, h * HD : (h + 1) * HD] = m
        squares = squares + m * m
        inner = inner + m * head(g, h).astype(f32)
    lane = lax.broadcasted_iota(jnp.int32, (T, HD), 1)
    both = jnp.where(
        lane == 0,
        jnp.sum(squares, axis=1, keepdims=True),
        jnp.where(lane == 1, jnp.sum(inner, axis=1, keepdims=True), 0.0),
    )
    rows = jnp.transpose(both)[0:8]
    for i in range(TP):
        sums[i] = rows


def norm_kernel(q, g, mix, sums, lin_out, grad_mix, own):
    rows = sums[0]
    for i in range(1, TP):
        rows = rows + sums[i]
    cols = jnp.transpose(jnp.concatenate([rows, jnp.zeros((T - 8, HD), f32)], axis=0))
    scale = lax.rsqrt(cols[:, 0:1] / (LH * HD) + epsilon)
    c = scale * cols[:, 1:2] / (LH * HD)
    for h in range(HERE):
        normed = head(mix, h) * scale
        lin_out[:, h * HD : (h + 1) * HD] = normed.astype(bf16)
        gm = (scale * (head(g, h).astype(f32) - normed * c)).astype(bf16)
        grad_mix[:, h * HD : (h + 1) * HD] = gm
        put_state(own, h, dot(head(q, h), gm, 0, 0))


def inside_kernel(q, k, v, gm, weights, s, grad_q, part_k, part_v):
    lower = lower_triangle()
    for h in range(HERE):
        at = slice(h * HD, (h + 1) * HD)
        gs = jnp.where(lower, dot(head(gm, h), head(v, h), 1, 1), 0.0).astype(bf16)
        gq = dot(gs, head(k, h), 1, 0) + dot(head(gm, h), state_of(s, h), 1, 1)
        grad_q[:, at] = gq.astype(bf16)
        part_k[:, at] = dot(gs, head(q, h), 0, 0)
        part_v[:, at] = dot(weights[h], head(gm, h), 0, 0)


def final_kernel(k, v, part_k, part_v, a, after, grad_k, grad_v):
    del after
    for h in range(HERE):
        at = slice(h * HD, (h + 1) * HD)
        later = state_of(a, h)
        grad_k[:, at] = (head(part_k, h) + dot(head(v, h), later, 1, 1)).astype(bf16)
        grad_v[:, at] = (head(part_v, h) + dot(head(k, h), later, 1, 0)).astype(bf16)


def soft_kernel(q_far, kv_far, doc_row, doc, out, ended, q, kv, qs, top, total, acc, sem, kv_sem):
    me = lax.axis_index("ctx")
    keys = CHUNK * T
    width = HERE * T
    factor = math.log2(math.e) / math.sqrt(HD)
    first_chunk = doc[0] // keys
    my_chunk = me // CHUNK
    last_start = doc[T - 1]

    def fetch(chunk):
        block = chunk * CHUNK
        source = kv_far.at[pl.ds(lax.rem(block, NZ), CHUNK), block // NZ]
        return pltpu.make_async_copy(source, kv.at[chunk], kv_sem.at[chunk])

    q_copy = pltpu.make_async_copy(q_far, q, sem)
    q_copy.start()

    def ask(chunk, carry):
        fetch(chunk).start()
        return carry

    lax.fori_loop(first_chunk, my_chunk + 1, ask, 0)
    q_copy.wait()
    for h in range(HERE):
        qs[h * T : (h + 1) * T] = head(q, h)
    top[...] = jnp.full((1, width), floor_score, f32)
    total[...] = jnp.zeros((1, width), f32)
    acc[...] = jnp.zeros((HD, width), f32)

    def visit(chunk, masked):
        k = kv[chunk, :, 0].reshape(keys, HD)
        v = kv[chunk, :, 1].reshape(keys, HD)
        scores = dot(k, qs[...], 1, 1)
        if masked:
            key_pos = chunk * keys + lax.broadcasted_iota(jnp.int32, (keys, width), 0)
            query_pos = me * T + lax.rem(
                lax.broadcasted_iota(jnp.int32, (1, width), 1), jnp.int32(T)
            )
            starts = jnp.concatenate([doc_row[...]] * HERE, axis=1)
            allowed = (key_pos <= query_pos) & (key_pos >= starts)
            scores = jnp.where(allowed, scores, 2 * floor_score)
        old_top = top[...]
        new_top = jnp.maximum(old_top, jnp.max(scores, axis=0, keepdims=True))
        probs = jnp.exp2((scores - new_top) * factor)
        shrink = jnp.exp2((old_top - new_top) * factor)
        top[...] = new_top
        total[...] = shrink * total[...] + jnp.sum(probs, axis=0, keepdims=True)
        acc[...] = shrink * acc[...] + dot(v, probs.astype(bf16), 0, 0)

    def step(chunk, carry):
        fetch(chunk).wait()
        clear = (chunk < my_chunk) & (chunk * keys >= last_start)

        @pl.when(clear)
        def _():
            visit(chunk, False)

        @pl.when(jnp.logical_not(clear))
        def _():
            visit(chunk, True)

        return carry

    lax.fori_loop(first_chunk, my_chunk + 1, step, 0)
    ended[...] = jnp.zeros((8, HD), f32)
    result = acc[...] / total[...]
    for h in range(HERE):
        out[:, h * HD : (h + 1) * HD] = jnp.transpose(result[:, h * T : (h + 1) * T]).astype(bf16)


def swap(pieces):
    return lax.all_to_all(pieces, "ctx", 0, 0, tiled=True, axis_index_groups=z_groups)


def carried_in(own, reverse):
    tag = "later" if reverse else "earlier"
    got = swap(own)
    (line,) = call(total_kernel, [((PIECE, HD), bf16)], got, flops=COST["total"], name=tag + "_total")
    sign = -1 if reverse else 1
    rows = [lax.ppermute(line, "ctx", y_shift(sign * s)) for s in (1, 2, 3)]
    (carried,) = call(
        functools.partial(carry_kernel, reverse),
        [((NZ, PIECE, HD), bf16)],
        got,
        *rows,
        flops=COST["carry"],
        name=tag + "_carry",
    )
    return swap(carried)


def on_device(
    lin_query, lin_key, lin_value, lin_cotangent, soft_query, soft_key, soft_value, doc_start
):
    wide = (T, HERE * HD)
    states = (NZ, PIECE, HD)
    squares = (HERE, T, T)
    dma = pltpu.SemaphoreType.DMA
    own, kv, k, v = call(
        own_kernel,
        [(states, bf16), ((NY, 2, T, HD), bf16), (wide, bf16), (wide, bf16)],
        lin_key,
        lin_value,
        soft_key,
        soft_value,
        far=(0, 1, 2, 3),
        flops=COST["own"],
        vmem=BIG,
        scratch=[dma((4,))],
        name="own_state",
    )
    line_kv = lax.all_to_all(kv, "ctx", 0, 0, tiled=True, axis_index_groups=y_groups)
    all_kv = lax.all_gather(line_kv, "ctx", axis_index_groups=z_groups)
    weights, local, q, g = call(
        local_kernel,
        [(squares, bf16), (wide, f32), (wide, bf16), (wide, bf16)],
        lin_query,
        lin_cotangent,
        k,
        v,
        far=(0, 1),
        scratch=[dma((2,))],
        flops=COST["local"], name="local",
    )
    earlier = carried_in(own, False)
    mix, sums = call(
        mix_kernel, [(wide, f32), ((TP, 8, HD), f32)], q, g, local, earlier, flops=COST["mix"], name="mix"
    )
    sums = lax.all_to_all(sums, "tp", 0, 0, tiled=True)
    lin_out, gm, own_adjoint = call(
        norm_kernel,
        [(wide, bf16), (wide, bf16), (states, bf16)],
        q,
        g,
        mix,
        sums,
        flops=COST["norm"], name="norm",
    )
    later = carried_in(own_adjoint, True)
    grad_query, part_k, part_v = call(
        inside_kernel,
        [(wide, bf16), (wide, f32), (wide, f32)],
        q,
        k,
        v,
        gm,
        weights,
        earlier,
        flops=COST["inside"], name="inside",
    )
    soft_out, ended = call(
        soft_kernel,
        [(wide, bf16), ((8, HD), f32)],
        soft_query,
        all_kv,
        doc_start.reshape(1, T),
        doc_start,
        smem=(3,),
        far=(0, 1),
        flops=COST["soft"],
        vmem=BIG,
        scratch=[
            pltpu.VMEM(wide, bf16),
            pltpu.VMEM((NY * NZ // CHUNK, CHUNK, 2, T, HD), bf16),
            pltpu.VMEM((HERE * T, HD), bf16),
            pltpu.VMEM((1, HERE * T), f32),
            pltpu.VMEM((1, HERE * T), f32),
            pltpu.VMEM((HD, HERE * T), f32),
            dma,
            dma((NY * NZ // CHUNK,)),
        ],
        name="soft",
    )
    grad_key, grad_value = call(
        final_kernel, [(wide, bf16), (wide, bf16)], k, v, part_k, part_v, later, ended, far=(5,), flops=COST["final"], name="final"
    )
    return (lin_out, grad_query, grad_key, grad_value, soft_out)


def solution(mesh):
    wide = P("ctx", "tp")
    return jax.shard_map(
        on_device,
        mesh=mesh,
        in_specs=(wide,) * 7 + (P("ctx"),),
        out_specs=(wide,) * 5,
        check_vma=False,
    )
```

```python
import functools
import math

import jax
import jax.numpy as jnp
from jax import lax
from jax.experimental import pallas as pl
from jax.experimental.pallas import tpu as pltpu
from jax.sharding import PartitionSpec as P

HD = 128
LH = 32
SH = 32
KVH = 8
T = 128
HERE = 4
TP = 8
NY = 4
NZ = 16
PIECE = HERE * HD // NZ
CHUNK = 4

BIG = 60 * 2**20
COST = dict(own=1e9, local=1e9, total=1e5, carry=1e5, mix=1e8, norm=1e8, inside=1e8, final=1e8, soft=1e8)

epsilon = 1e-06
floor_score = -1e30
bf16 = jnp.bfloat16
f32 = jnp.float32

y_groups = [[y * NZ + z for y in range(NY)] for z in range(NZ)]
z_groups = [[y * NZ + z for z in range(NZ)] for y in range(NY)]


def y_shift(step):
    return [(i, i + NZ * step) for i in range(NY * NZ) if 0 <= i + NZ * step < NY * NZ]


def dot(a, b, contract_a, contract_b):
    return lax.dot_general(
        a, b, (((contract_a,), (contract_b,)), ((), ())), preferred_element_type=f32
    )


def call(kernel, outs, *args, flops=1e8, name=None, vmem=16 * 2**20, scratch=(), smem=(), far=(), far_out=(), smem_out=()):
    size = sum(a.size * a.dtype.itemsize for a in args)
    size += sum(math.prod(s) * jnp.dtype(d).itemsize for s, d in outs)
    specs = [
        pl.BlockSpec(memory_space=pltpu.SMEM if i in smem else pltpu.HBM if i in far else pltpu.VMEM)
        for i in range(len(args))
    ]
    out = pl.pallas_call(
        kernel,
        out_shape=[jax.ShapeDtypeStruct(s, d) for s, d in outs],
        in_specs=specs,
        out_specs=[
            pl.BlockSpec(
                memory_space=pltpu.HBM if i in far_out else pltpu.SMEM if i in smem_out else pltpu.VMEM
            )
            for i in range(len(outs))
        ],
        scratch_shapes=list(scratch),
        compiler_params=pltpu.CompilerParams(vmem_limit_bytes=vmem),
        cost_estimate=pl.CostEstimate(flops=int(flops), bytes_accessed=size, transcendentals=0),
        name=name,
    )(*args)
    return out


def head(ref, h):
    return ref[:, h * HD : (h + 1) * HD]


def state_of(ref, h):
    per = HD // PIECE
    return ref[h * per : (h + 1) * per].reshape(HD, HD)


def put_state(ref, h, value):
    per = HD // PIECE
    ref[h * per : (h + 1) * per] = value.astype(bf16).reshape(per, PIECE, HD)


def lower_triangle():
    rows = lax.broadcasted_iota(jnp.int32, (T, T), 0)
    cols = lax.broadcasted_iota(jnp.int32, (T, T), 1)
    return cols <= rows


def own_kernel(k_far, v_far, sk_far, sv_far, own, kv, k, v, sem):
    moves = [(k_far, k), (v_far, v), (sk_far, kv.at[0, 0]), (sv_far, kv.at[0, 1])]
    copies = [pltpu.make_async_copy(a, b, sem.at[i]) for i, (a, b) in enumerate(moves)]
    for copy in copies:
        copy.start()
    copies[0].wait()
    copies[1].wait()
    for h in range(HERE):
        put_state(own, h, dot(head(k, h), head(v, h), 0, 0))
    copies[2].wait()
    copies[3].wait()
    for y in range(1, NY):
        kv[y] = kv[0]


def local_kernel(q_far, g_far, k, v, weights, local, q, g, sem):
    moves = [(q_far, q), (g_far, g)]
    copies = [pltpu.make_async_copy(a, b, sem.at[i]) for i, (a, b) in enumerate(moves)]
    for copy in copies:
        copy.start()
    for copy in copies:
        copy.wait()
    lower = lower_triangle()
    for h in range(HERE):
        w = jnp.where(lower, dot(head(q, h), head(k, h), 1, 1), 0.0).astype(bf16)
        weights[h] = w
        local[:, h * HD : (h + 1) * HD] = dot(w, head(v, h), 1, 0)


def total_kernel(r, after, tot):
    del after
    acc = r[0].astype(f32)
    for i in range(1, NZ):
        acc = acc + r[i].astype(f32)
    tot[...] = acc.astype(bf16)


def carry_kernel(reverse, r, a, b, c, out):
    acc = a[...].astype(f32) + b[...].astype(f32) + c[...].astype(f32)
    for i in reversed(range(NZ)) if reverse else range(NZ):
        out[i] = acc.astype(bf16)
        acc = acc + r[i].astype(f32)


def mix_kernel(q, g, local, s, mix, sums):
    squares = jnp.zeros((T, HD), f32)
    inner = jnp.zeros((T, HD), f32)
    for h in range(HERE):
        m = head(local, h) + dot(head(q, h), state_of(s, h), 1, 0)
        mix[:, h * HD : (h + 1) * HD] = m
        squares = squares + m * m
        inner = inner + m * head(g, h).astype(f32)
    lane = lax.broadcasted_iota(jnp.int32, (T, HD), 1)
    both = jnp.where(
        lane == 0,
        jnp.sum(squares, axis=1, keepdims=True),
        jnp.where(lane == 1, jnp.sum(inner, axis=1, keepdims=True), 0.0),
    )
    rows = jnp.transpose(both)[0:8]
    for i in range(TP):
        sums[i] = rows


def norm_kernel(q, g, mix, sums, lin_out, grad_mix, own):
    rows = sums[0]
    for i in range(1, TP):
        rows = rows + sums[i]
    cols = jnp.transpose(jnp.concatenate([rows, jnp.zeros((T - 8, HD), f32)], axis=0))
    scale = lax.rsqrt(cols[:, 0:1] / (LH * HD) + epsilon)
    c = scale * cols[:, 1:2] / (LH * HD)
    for h in range(HERE):
        normed = head(mix, h) * scale
        lin_out[:, h * HD : (h + 1) * HD] = normed.astype(bf16)
        gm = (scale * (head(g, h).astype(f32) - normed * c)).astype(bf16)
        grad_mix[:, h * HD : (h + 1) * HD] = gm
        put_state(own, h, dot(head(q, h), gm, 0, 0))


def inside_kernel(q, k, v, gm, weights, s, grad_q, part_k, part_v):
    lower = lower_triangle()
    for h in range(HERE):
        at = slice(h * HD, (h + 1) * HD)
        gs = jnp.where(lower, dot(head(gm, h), head(v, h), 1, 1), 0.0).astype(bf16)
        gq = dot(gs, head(k, h), 1, 0) + dot(head(gm, h), state_of(s, h), 1, 1)
        grad_q[:, at] = gq.astype(bf16)
        part_k[:, at] = dot(gs, head(q, h), 0, 0)
        part_v[:, at] = dot(weights[h], head(gm, h), 0, 0)


def final_kernel(k, v, part_k, part_v, a, after, grad_k, grad_v):
    del after
    for h in range(HERE):
        at = slice(h * HD, (h + 1) * HD)
        later = state_of(a, h)
        grad_k[:, at] = (head(part_k, h) + dot(head(v, h), later, 1, 1)).astype(bf16)
        grad_v[:, at] = (head(part_v, h) + dot(head(k, h), later, 1, 0)).astype(bf16)


def soft_kernel(q_far, kv_far, doc_row, doc, out, ended, q, kv, qs, top, total, acc, sem, kv_sem):
    me = lax.axis_index("ctx")
    keys = CHUNK * T
    width = HERE * T
    factor = math.log2(math.e) / math.sqrt(HD)
    first_chunk = doc[0] // keys
    my_chunk = me // CHUNK
    last_start = doc[T - 1]

    def fetch(chunk):
        block = chunk * CHUNK
        source = kv_far.at[pl.ds(lax.rem(block, NZ), CHUNK), block // NZ]
        return pltpu.make_async_copy(source, kv.at[chunk], kv_sem.at[chunk])

    q_copy = pltpu.make_async_copy(q_far, q, sem)
    q_copy.start()

    def ask(chunk, carry):
        fetch(chunk).start()
        return carry

    lax.fori_loop(first_chunk, my_chunk + 1, ask, 0)
    q_copy.wait()
    for h in range(HERE):
        qs[h * T : (h + 1) * T] = head(q, h)
    top[...] = jnp.full((1, width), floor_score, f32)
    total[...] = jnp.zeros((1, width), f32)
    acc[...] = jnp.zeros((HD, width), f32)

    def visit(chunk, masked):
        k = kv[chunk, :, 0].reshape(keys, HD)
        v = kv[chunk, :, 1].reshape(keys, HD)
        scores = dot(k, qs[...], 1, 1)
        if masked:
            key_pos = chunk * keys + lax.broadcasted_iota(jnp.int32, (keys, width), 0)
            query_pos = me * T + lax.rem(
                lax.broadcasted_iota(jnp.int32, (1, width), 1), jnp.int32(T)
            )
            starts = jnp.concatenate([doc_row[...]] * HERE, axis=1)
            allowed = (key_pos <= query_pos) & (key_pos >= starts)
            scores = jnp.where(allowed, scores, 2 * floor_score)
        old_top = top[...]
        new_top = jnp.maximum(old_top, jnp.max(scores, axis=0, keepdims=True))
        probs = jnp.exp2((scores - new_top) * factor)
        shrink = jnp.exp2((old_top - new_top) * factor)
        top[...] = new_top
        total[...] = shrink * total[...] + jnp.sum(probs, axis=0, keepdims=True)
        acc[...] = shrink * acc[...] + dot(v, probs.astype(bf16), 0, 0)

    def step(chunk, carry):
        fetch(chunk).wait()
        clear = (chunk < my_chunk) & (chunk * keys >= last_start)

        @pl.when(clear)
        def _():
            visit(chunk, False)

        @pl.when(jnp.logical_not(clear))
        def _():
            visit(chunk, True)

        return carry

    lax.fori_loop(first_chunk, my_chunk + 1, step, 0)
    ended[0] = my_chunk
    result = acc[...] / total[...]
    for h in range(HERE):
        out[:, h * HD : (h + 1) * HD] = jnp.transpose(result[:, h * T : (h + 1) * T]).astype(bf16)


def swap(pieces):
    return lax.all_to_all(pieces, "ctx", 0, 0, tiled=True, axis_index_groups=z_groups)


def carried_in(own, after, reverse):
    tag = "later" if reverse else "earlier"
    got = swap(own)
    (line,) = call(total_kernel, [((PIECE, HD), bf16)], got, after, flops=COST["total"], name=tag + "_total")
    sign = -1 if reverse else 1
    rows = [lax.ppermute(line, "ctx", y_shift(sign * s)) for s in (1, 2, 3)]
    (carried,) = call(
        functools.partial(carry_kernel, reverse),
        [((NZ, PIECE, HD), bf16)],
        got,
        *rows,
        flops=COST["carry"],
        name=tag + "_carry",
    )
    return swap(carried)


def on_device(
    lin_query, lin_key, lin_value, lin_cotangent, soft_query, soft_key, soft_value, doc_start
):
    wide = (T, HERE * HD)
    states = (NZ, PIECE, HD)
    squares = (HERE, T, T)
    dma = pltpu.SemaphoreType.DMA
    own, kv, k, v = call(
        own_kernel,
        [(states, bf16), ((NY, 2, T, HD), bf16), (wide, bf16), (wide, bf16)],
        lin_key,
        lin_value,
        soft_key,
        soft_value,
        far=(0, 1, 2, 3),
        flops=COST["own"],
        vmem=BIG,
        scratch=[dma((4,))],
        name="own_state",
    )
    line_kv = lax.all_to_all(kv, "ctx", 0, 0, tiled=True, axis_index_groups=y_groups)
    all_kv = lax.all_gather(line_kv, "ctx", axis_index_groups=z_groups)
    weights, local, q, g = call(
        local_kernel,
        [(squares, bf16), (wide, f32), (wide, bf16), (wide, bf16)],
        lin_query,
        lin_cotangent,
        k,
        v,
        far=(0, 1),
        scratch=[dma((2,))],
        flops=COST["local"], name="local",
    )
    earlier = carried_in(own, local, False)
    mix, sums = call(
        mix_kernel, [(wide, f32), ((TP, 8, HD), f32)], q, g, local, earlier, flops=COST["mix"], name="mix"
    )
    sums = lax.all_to_all(sums, "tp", 0, 0, tiled=True)
    lin_out, gm, own_adjoint = call(
        norm_kernel,
        [(wide, bf16), (wide, bf16), (states, bf16)],
        q,
        g,
        mix,
        sums,
        flops=COST["norm"], name="norm",
    )
    grad_query, part_k, part_v = call(
        inside_kernel,
        [(wide, bf16), (wide, f32), (wide, f32)],
        q,
        k,
        v,
        gm,
        weights,
        earlier,
        flops=COST["inside"], name="inside",
    )
    later = carried_in(own_adjoint, part_k, True)
    soft_out, ended = call(
        soft_kernel,
        [(wide, bf16), ((1,), jnp.int32)],
        soft_query,
        all_kv,
        doc_start.reshape(1, T),
        doc_start,
        smem=(3,),
        smem_out=(1,),
        far=(0, 1),
        flops=COST["soft"],
        vmem=BIG,
        scratch=[
            pltpu.VMEM(wide, bf16),
            pltpu.VMEM((NY * NZ // CHUNK, CHUNK, 2, T, HD), bf16),
            pltpu.VMEM((HERE * T, HD), bf16),
            pltpu.VMEM((1, HERE * T), f32),
            pltpu.VMEM((1, HERE * T), f32),
            pltpu.VMEM((HD, HERE * T), f32),
            dma,
            dma((NY * NZ // CHUNK,)),
        ],
        name="soft",
    )
    grad_key, grad_value = call(
        final_kernel, [(wide, bf16), (wide, bf16)], k, v, part_k, part_v, later, ended, smem=(5,), flops=COST["final"], name="final"
    )
    return (lin_out, grad_query, grad_key, grad_value, soft_out)


def solution(mesh):
    wide = P("ctx", "tp")
    return jax.shard_map(
        on_device,
        mesh=mesh,
        in_specs=(wide,) * 7 + (P("ctx"),),
        out_specs=(wide,) * 5,
        check_vma=False,
    )
```
